32 devices in a mesh: row: 4 (over z), col: 8 (over y, x, core).
Axes of the slice: x: 2, y: 2, z: 4, core: 2. Of those that a mesh axis runs over, the one named last changes fastest.
Arguments:
- colloc_points: float32 [3, 61440], P(None, 'row'), may hold values from -1 to 1, as said below
- sources: float32 [4, 1024], P(None, 'col'), may hold values from -1 to 1, as said below
- counts: int32 [480, 8], P('row', 'col'), may hold values from 2 to 16, as said below
- row_element: int32 [61440], P('row'), may hold values from 0 to 61439, as said below
- pivots: int32 [128], replicated, may hold values from 0 to 61439, as said below
Outputs:
- factored: float32 [61440, 1024], P('row', 'col')
- u_rows: float32 [128, 1024], P(None, 'col')
The draws below stay inside these ranges and needn't reach their ends.
Inputs may be any that keep to these rules, and one draw needn't show every extreme that they name: `counts`: every tile uses 2 to 16 quadrature points, and some tile uses 16. `row_element`: a permutation of the 61440 elements. pivots[k] is the row r with row_element[r] == k. `colloc_points`: first two coordinates between 0 and 1, third between -0.1 and 0.1. `sources`: centres as for the collocation points; core radii between 0.05 and 0.15.
All inputs are finite; a program needn't handle non-finite values.
Results may differ from the reference program's by a relative error of at most 0.0003.
Values sent between devices are 32-bit elements; how exact they have to be, the bound alone decides.
A program may use at most 64 MiB of HBM per device.

```python
import jax
import jax.numpy as jnp
from jax import lax

MATRIX_ORDER = 61440
TILE_SIZE = 128
QUAD_MAX = 16
TILE_COLS_DEV = 1
TILE_ROWS_DEV = 120
ROW_TILES = 480
COL_TILES = 8
WINDOW_COLS = 1024


def element_order(key):
    return jax.random.permutation(jax.random.fold_in(key, 11), MATRIX_ORDER).astype(jnp.int32)


def draw_row_element(key, part):
    return element_order(key)


def draw_pivots(key, part):
    ordering = element_order(key)
    return jnp.argsort(ordering, stable=True)[:TILE_SIZE].astype(jnp.int32)


def surface_points(key, amount):
    subkeys = jax.random.split(jax.random.fold_in(key, 23), 2)
    plane = jax.random.uniform(subkeys[0], (2, amount), jnp.float32)
    height = jax.random.uniform(subkeys[1], (1, amount), jnp.float32, -0.1, 0.1)
    return jnp.concatenate([plane, height], 0)


def draw_colloc_points(key, part):
    return surface_points(key, MATRIX_ORDER)


def draw_sources(key, part):
    centres = surface_points(jax.random.fold_in(key, 5), WINDOW_COLS)
    logs = jax.random.uniform(jax.random.fold_in(key, 7), (1, WINDOW_COLS), jnp.float32, jnp.log(0.05), jnp.log(0.15))
    sizes = jnp.exp(logs)
    return jnp.concatenate([centres, sizes], 0)


def draw_counts(key, part):
    subkeys = jax.random.split(jax.random.fold_in(key, 31), 4)
    drawn = jax.random.randint(subkeys[0], (ROW_TILES, COL_TILES), 2, 7)
    near_tip = jax.random.randint(subkeys[1], (ROW_TILES, COL_TILES), 12, QUAD_MAX + 1)
    band_row = jax.random.randint(subkeys[2], (), 0, ROW_TILES // TILE_ROWS_DEV)
    band_col = jax.random.randint(subkeys[3], (), 0, COL_TILES // TILE_COLS_DEV)
    rows_group = jnp.arange(ROW_TILES)[:, None] // TILE_ROWS_DEV
    cols_group = jnp.arange(COL_TILES)[None, :] // TILE_COLS_DEV
    in_region = (rows_group == band_row) & (cols_group == band_col)
    tiles = jnp.where(in_region, near_tip, drawn)
    tiles = tiles.at[band_row * TILE_ROWS_DEV, band_col * TILE_COLS_DEV].set(QUAD_MAX)
    return tiles.astype(jnp.int32)


def setup_inputs(seed: int = 0) -> dict:
    splits = jax.random.split(jax.random.key(seed), 6)
    return {
        "colloc_points": draw_colloc_points(jax.random.fold_in(splits[5], 71), 0),
        "sources": draw_sources(jax.random.fold_in(splits[5], 71), 0),
        "counts": draw_counts(jax.random.fold_in(splits[5], 71), 0),
        "row_element": draw_row_element(jax.random.fold_in(splits[5], 71), 0),
        "pivots": draw_pivots(jax.random.fold_in(splits[5], 71), 0),
    }


jump_factor = 4.0
disc_radius = 4.0

def quad_offsets():
    numbers = jnp.arange(QUAD_MAX).astype(jnp.float32)
    radius = disc_radius * jnp.sqrt((numbers + 0.5) / QUAD_MAX)
    angles = 2.39996323 * numbers
    return (radius * jnp.cos(angles), radius * jnp.sin(angles))

def kelvin_entry(point_x, point_y, point_z, source_x, source_y, source_z, source_size):
    delta_x = point_x - source_x
    delta_y = point_y - source_y
    delta_z = point_z - source_z
    rho_sq = delta_x * delta_x + delta_y * delta_y + delta_z * delta_z + source_size * source_size
    return (2.0 + delta_z * delta_z / rho_sq) * lax.rsqrt(rho_sq)

def lower_unit_inverse(lower_unit):
    side = lower_unit.shape[0]
    positions = jnp.arange(side)
    strict = jnp.tril(lower_unit, -1)

    def step(index, inverse):
        unit_row = (positions == index).astype(inverse.dtype)
        strict_row = lax.dynamic_index_in_dim(strict, index, 0, keepdims=False)
        new_row = unit_row - jnp.dot(strict_row, inverse, precision=lax.Precision.HIGHEST)
        return lax.dynamic_update_index_in_dim(inverse, new_row, index, 0)
    return lax.fori_loop(0, side, step, jnp.zeros_like(lower_unit))

def upper_inverse(upper_part):
    side = upper_part.shape[0]
    positions = jnp.arange(side)
    strict = jnp.triu(upper_part, 1)

    def step(count, inverse):
        index = side - 1 - count
        unit_row = (positions == index).astype(inverse.dtype)
        strict_row = lax.dynamic_index_in_dim(strict, index, 0, keepdims=False)
        full_row = lax.dynamic_index_in_dim(upper_part, index, 0, keepdims=False)
        pivot_value = lax.dynamic_index_in_dim(full_row, index, 0, keepdims=False)
        new_row = (unit_row - jnp.dot(strict_row, inverse, precision=lax.Precision.HIGHEST)) / pivot_value
        return lax.dynamic_update_index_in_dim(inverse, new_row, index, 0)
    return lax.fori_loop(0, side, step, jnp.zeros_like(upper_part))

def factor_square(square):
    side = square.shape[0]
    positions = jnp.arange(side)

    def eliminate(column, packed):
        pivot_row = lax.dynamic_index_in_dim(packed, column, 0, keepdims=False)
        pivot_col = lax.dynamic_index_in_dim(packed, column, 1, keepdims=False)
        pivot_value = lax.dynamic_index_in_dim(pivot_row, column, 0, keepdims=False)
        under_mask = positions > column
        factor = jnp.where(under_mask, pivot_col / pivot_value, 0.0)
        right_row = jnp.where(under_mask, pivot_row, 0.0)
        packed = packed - factor[:, None] * right_row[None, :]
        return jnp.where((positions[None, :] == column) & under_mask[:, None], factor[:, None], packed)
    return lax.fori_loop(0, side, eliminate, square)

def factor_panel(square):
    panel_size = square.shape[0]
    block_width = min(16, panel_size)
    identity = jnp.eye(block_width, dtype=square.dtype)
    packed = square
    for first_col in range(0, panel_size, block_width):
        last_col = first_col + block_width
        diagonal = factor_square(packed[first_col:last_col, first_col:last_col])
        packed = packed.at[first_col:last_col, first_col:last_col].set(diagonal)
        if last_col < panel_size:
            lower_unit = jnp.tril(diagonal, -1) + identity
            upper_part = jnp.triu(diagonal)
            upper_inv = upper_inverse(upper_part)
            lower_inv = lower_unit_inverse(lower_unit)
            left_part = jnp.dot(packed[last_col:, first_col:last_col], upper_inv, precision=lax.Precision.HIGHEST)
            top_part = jnp.dot(lower_inv, packed[first_col:last_col, last_col:], precision=lax.Precision.HIGHEST)
            packed = packed.at[last_col:, first_col:last_col].set(left_part)
            packed = packed.at[first_col:last_col, last_col:].set(top_part)
            packed = packed.at[last_col:, last_col:].add(-jnp.dot(left_part, top_part, precision=lax.Precision.HIGHEST))
    return packed

def triangle_inverses(square):
    identity = jnp.eye(square.shape[0], dtype=square.dtype)
    packed = factor_panel(square)
    lower_unit = jnp.tril(packed, -1) + identity
    upper_part = jnp.triu(packed)
    return (upper_inverse(upper_part), lower_unit_inverse(lower_unit))

def reference(colloc_points, sources, counts, row_element, pivots):
    offset_x, offset_y = quad_offsets()

    def one_panel(column_tile):
        source = lax.dynamic_slice_in_dim(sources, column_tile * TILE_SIZE, TILE_SIZE, 1)
        tile_counts = lax.dynamic_index_in_dim(counts, column_tile, 1, keepdims=False)
        row_counts = jnp.repeat(tile_counts, TILE_SIZE, total_repeat_length=MATRIX_ORDER).astype(jnp.float32)
        running = jnp.zeros((MATRIX_ORDER, TILE_SIZE), jnp.float32)
        for quad_index in range(QUAD_MAX):
            weight = jnp.where(quad_index < row_counts, 1.0 / row_counts, 0.0)
            kernel_values = kelvin_entry(colloc_points[0][:, None], colloc_points[1][:, None], colloc_points[2][:, None], (source[0] + source[3] * offset_x[quad_index])[None, :], (source[1] + source[3] * offset_y[quad_index])[None, :], source[2][None, :], source[3][None, :])
            running = running + weight[:, None] * kernel_values
        return running
    panels = lax.map(one_panel, jnp.arange(COL_TILES))
    assembled = jnp.transpose(panels, (1, 0, 2)).reshape(MATRIX_ORDER, WINDOW_COLS)
    jump = jump_factor * TILE_SIZE
    column_ids = jnp.arange(WINDOW_COLS).astype(jnp.int32)
    matrix = assembled + jump * (row_element[:, None] == column_ids[None, :]).astype(jnp.float32)
    pivot_block = matrix[pivots]
    upper_inv, lower_inv = triangle_inverses(pivot_block[:, :TILE_SIZE])
    panel_factor = jnp.dot(matrix[:, :TILE_SIZE], upper_inv, precision=lax.Precision.HIGHEST, preferred_element_type=jnp.float32)
    u_rows = jnp.dot(lower_inv, pivot_block, precision=lax.Precision.HIGHEST, preferred_element_type=jnp.float32)
    factored = matrix - jnp.dot(panel_factor, u_rows, precision=lax.Precision.HIGHEST, preferred_element_type=jnp.float32)
    factored = factored.at[:, :TILE_SIZE].set(panel_factor)
    return (factored, u_rows)
```

```python
import functools
import math

import jax
import jax.numpy as jnp
from jax import lax
from jax.experimental import pallas as pl
from jax.experimental.pallas import tpu as pltpu
from jax.sharding import PartitionSpec as P

QUAD_MAX = 16
jump_factor = 4.0
disc_radius = 4.0

offset_x = [
    disc_radius * math.sqrt((q + 0.5) / QUAD_MAX) * math.cos(2.39996323 * q) for q in range(QUAD_MAX)
]
offset_y = [
    disc_radius * math.sqrt((q + 0.5) / QUAD_MAX) * math.sin(2.39996323 * q) for q in range(QUAD_MAX)
]


def fill_tables(src_ref, table_x, table_y):
    size = src_ref[3:4, :]
    for q in range(QUAD_MAX):
        table_x[q : q + 1, :] = src_ref[0:1, :] + size * offset_x[q]
        table_y[q : q + 1, :] = src_ref[1:2, :] + size * offset_y[q]


def tile_matrix(feat, src_ref, table_x, table_y, count, first_column, jump):
    tile = feat.shape[1]
    columns = jnp.transpose(feat)
    shape = (tile, src_ref.shape[1])
    point_x = jnp.broadcast_to(columns[:, 0:1], shape)
    point_y = jnp.broadcast_to(columns[:, 1:2], shape)
    delta_z = columns[:, 2:3] - src_ref[2:3, :]
    z_sq = delta_z * delta_z
    size = src_ref[3:4, :]
    base = z_sq + size * size

    def add_point(q, sums):
        first, third = sums
        delta_x = point_x - table_x[pl.ds(q, 1), :]
        delta_y = point_y - table_y[pl.ds(q, 1), :]
        inverse = lax.rsqrt(delta_x * delta_x + delta_y * delta_y + base)
        return first + inverse, third + inverse * inverse * inverse

    def add_two(pair, sums):
        return add_point(2 * pair + 1, add_point(2 * pair, sums))

    zero = jnp.zeros(shape, jnp.float32)
    sums = lax.fori_loop(0, count // 2, add_two, (zero, zero))
    first, third = lax.fori_loop(count // 2 * 2, count, add_point, sums)
    weight = 1.0 / jnp.full((1, shape[1]), count, jnp.int32).astype(jnp.float32)
    values = (2.0 * first + z_sq * third) * weight
    lanes = lax.broadcasted_iota(jnp.int32, (1, shape[1]), 1) + first_column
    hit = columns[:, 3:4] == lanes.astype(jnp.float32)
    return values + jnp.where(hit, jump, 0.0)


def assemble_kernel(group, tile, jump, place_ref, counts_ref, feat_ref, src_ref, out_ref, table_x, table_y):
    step = pl.program_id(0)

    @pl.when(step == 0)
    def _():
        fill_tables(src_ref, table_x, table_y)

    def one_tile(index, carry):
        start = pl.multiple_of(index * tile, tile)
        out_ref[pl.ds(start, tile), :] = tile_matrix(
            feat_ref[:, pl.ds(start, tile)],
            src_ref,
            table_x,
            table_y,
            counts_ref[step * group + index],
            place_ref[0],
            jump,
        )
        return carry

    lax.fori_loop(0, group, one_tile, 0)


def split_two(value):
    high = value.astype(jnp.bfloat16)
    low = (value - high.astype(jnp.float32)).astype(jnp.bfloat16)
    return high, low


def update_kernel(
    group, tile, jump, place_ref, counts_ref, feat_ref, src_ref, gain_ref, own_ref, out_ref,
    table_x, table_y, gain_wide, gain_high,
):
    step = pl.program_id(0)

    @pl.when(step == 0)
    def _():
        fill_tables(src_ref, table_x, table_y)
        high, low = split_two(gain_ref[...])
        gain_wide[:, :tile] = high
        gain_wide[:, tile:] = low
        gain_high[...] = high

    keep = jnp.where(place_ref[0] == 0, 0.0, 1.0)

    def one_tile(index, carry):
        start = pl.multiple_of(index * tile, tile)
        panel = tile_matrix(
            feat_ref[:, pl.ds(start, tile)],
            src_ref,
            table_x,
            table_y,
            counts_ref[step * group + index],
            0,
            jump,
        )
        high, low = split_two(panel)
        wide = jnp.dot(high, gain_wide[...], preferred_element_type=jnp.float32)
        small = jnp.dot(low, gain_high[...], preferred_element_type=jnp.float32)
        product = wide[:, :tile] + (wide[:, tile:] + small)
        out_ref[pl.ds(start, tile), :] = keep * own_ref[pl.ds(start, tile), :] + product
        return carry

    lax.fori_loop(0, group, one_tile, 0)


def pivot_matrix(columns, src_ref, counts):
    delta_x = columns[:, 0:1] - src_ref[0:1, :]
    delta_y = columns[:, 1:2] - src_ref[1:2, :]
    delta_z = columns[:, 2:3] - src_ref[2:3, :]
    size = src_ref[3:4, :]
    z_sq = delta_z * delta_z
    base = z_sq + size * size
    total = jnp.zeros_like(base)
    for q in range(QUAD_MAX):
        moved_x = delta_x - size * offset_x[q]
        moved_y = delta_y - size * offset_y[q]
        inverse = lax.rsqrt(moved_x * moved_x + moved_y * moved_y + base)
        weight = jnp.where(counts > q, 1.0 / counts, 0.0)
        total = total + weight * ((2.0 + z_sq * inverse * inverse) * inverse)
    return total


def eliminated(blocks, lanes, steps):
    rows = lax.broadcasted_iota(jnp.int32, (8, 1), 0)
    for column in steps:
        group, inner = divmod(column, 8)
        for blocks_of in blocks:
            pivot_row = blocks_of[group][inner : inner + 1, :]
            scale = 1.0 / pivot_row[:, column : column + 1]
            here = lanes == column
            right_row = jnp.where(here, 1.0, pivot_row)
            for index in range(group, len(blocks_of)):
                block = blocks_of[index]
                factor = block[:, column : column + 1] * scale
                if index == group:
                    under = rows > inner
                    factor = jnp.where(under, factor, 0.0)
                    cleared = jnp.where(here & under, 0.0, block)
                else:
                    cleared = jnp.where(here, 0.0, block)
                blocks_of[index] = cleared - factor * right_row
    return blocks


def panel_kernel(jump, place_ref, piv_ref, own_ref, root_ref, u_ref, gain_ref):
    side = piv_ref.shape[1]
    columns = jnp.transpose(piv_ref[...])
    rows = lax.broadcasted_iota(jnp.int32, (side, side), 0)
    cols = lax.broadcasted_iota(jnp.int32, (side, side), 1)
    diagonal = rows == cols
    is_root = place_ref[0] == 0
    identity = jnp.where(diagonal, 1.0, 0.0)
    square = pivot_matrix(columns, root_ref, columns[:, 4:5]) + jump * identity
    own = pivot_matrix(columns, own_ref, columns[:, 3:4]) + jnp.where(is_root, jump, 0.0) * identity
    lanes = lax.broadcasted_iota(jnp.int32, (1, side), 1)
    flipped = jnp.transpose(square)
    blocks = [
        [square[i : i + 8, :] for i in range(0, side, 8)],
        [flipped[i : i + 8, :] for i in range(0, side, 8)],
    ]
    blocks = eliminated(blocks, lanes, range(side))
    packed = jnp.concatenate(blocks[0], 0)
    packed_flipped = jnp.concatenate(blocks[1], 0)
    lower_inv = jnp.where(rows > cols, packed, identity)
    pivot_values = jnp.sum(jnp.where(diagonal, packed_flipped, 0.0), axis=1, keepdims=True)
    upper_inv = jnp.transpose(jnp.where(rows > cols, packed_flipped, identity) / pivot_values)
    u_rows = jnp.dot(
        lower_inv, own, precision=lax.Precision.HIGHEST, preferred_element_type=jnp.float32
    )
    u_ref[...] = u_rows
    gain = jnp.dot(
        upper_inv, u_rows, precision=lax.Precision.HIGHEST, preferred_element_type=jnp.float32
    )
    gain_ref[...] = jnp.where(is_root, upper_inv, -gain)


def body(colloc_points, sources, counts, row_element, pivots):
    tile = pivots.shape[0]
    local_rows = colloc_points.shape[1]
    local_cols = sources.shape[1]
    rows_tiles = local_rows // tile
    col_index = lax.axis_index("col")
    row_index = lax.axis_index("row")
    col_count = lax.axis_size("col")
    row_count = lax.axis_size("row")
    jump = jump_factor * tile
    own_counts = counts.reshape(-1)
    place = (col_index * local_cols).astype(jnp.int32).reshape(1)

    local_ids = pivots - row_index * local_rows
    present = (local_ids >= 0) & (local_ids < local_rows)
    local_ids = jnp.clip(local_ids, 0, local_rows - 1)
    real_counts = own_counts.astype(jnp.float32)
    pivot_points = jnp.where(present & (col_index == 0), colloc_points[:, local_ids], 0.0)
    pivot_counts = jnp.where(present, real_counts[local_ids // tile], 0.0)
    root_sources = jnp.where((row_index == 0) & (col_index == 0), sources, 0.0)
    spread_counts = jnp.where(jnp.arange(col_count)[:, None] == col_index, pivot_counts[None, :], 0.0)
    padded = jnp.pad(real_counts, (0, -rows_tiles % tile))
    depth = padded.shape[0] // tile
    at_row = (jnp.arange(row_count)[:, None] == row_index) & (col_index == 0)
    root_counts = jnp.where(at_row, padded[None, :], 0.0).reshape(row_count * depth, tile)
    packed = jnp.concatenate([pivot_points, root_sources, spread_counts, root_counts], 0)
    known = lax.psum(packed, ("row", "col"))
    pivot_points = known[0:3]
    root_sources = known[3:7]
    spread_counts = known[7 : 7 + col_count]
    own_pivot_counts = lax.dynamic_index_in_dim(spread_counts, col_index, 0)
    root_counts = known[7 + col_count :].reshape(row_count, depth * tile)
    root_counts = lax.dynamic_index_in_dim(root_counts, row_index, 0, keepdims=False)
    root_counts = jnp.round(root_counts[:rows_tiles]).astype(jnp.int32)
    pivot_info = jnp.concatenate(
        [pivot_points, own_pivot_counts, spread_counts[0:1], jnp.zeros((3, tile), jnp.float32)], 0
    )

    features = jnp.concatenate(
        [
            colloc_points,
            row_element.astype(jnp.float32)[None, :],
            jnp.zeros((4, local_rows), jnp.float32),
        ],
        0,
    )
    group = max(size for size in range(1, 9) if rows_tiles % size == 0)
    steps = rows_tiles // group
    scalar = pl.BlockSpec(memory_space=pltpu.SMEM)
    whole = pl.BlockSpec(memory_space=pltpu.VMEM)
    feature_block = pl.BlockSpec((8, group * tile), lambda i: (0, i))
    matrix_block = pl.BlockSpec((group * tile, local_cols), lambda i: (i, 0))
    tables = [pltpu.VMEM((QUAD_MAX, local_cols), jnp.float32)] * 2
    params = pltpu.CompilerParams(vmem_limit_bytes=24 * 1024 * 1024)
    block = jax.ShapeDtypeStruct((local_rows, local_cols), jnp.float32)
    work = local_rows * local_cols

    matrix = pl.pallas_call(
        functools.partial(assemble_kernel, group, tile, jump),
        grid=(steps,),
        out_shape=block,
        in_specs=[scalar, scalar, feature_block, whole],
        out_specs=matrix_block,
        scratch_shapes=tables,
        compiler_params=params,
        cost_estimate=pl.CostEstimate(
            flops=work * 80, bytes_accessed=work * 4, transcendentals=work * 6
        ),
        name="assemble",
    )(place, own_counts, features, sources)

    u_rows, gain = pl.pallas_call(
        functools.partial(panel_kernel, jump),
        out_shape=[jax.ShapeDtypeStruct((tile, local_cols), jnp.float32)] * 2,
        in_specs=[scalar, whole, whole, whole],
        out_specs=[whole, whole],
        compiler_params=params,
        name="panel",
    )(place, pivot_info, sources, root_sources)

    factored = pl.pallas_call(
        functools.partial(update_kernel, group, tile, jump),
        grid=(steps,),
        out_shape=block,
        in_specs=[scalar, scalar, feature_block, whole, whole, matrix_block],
        out_specs=matrix_block,
        scratch_shapes=tables
        + [pltpu.VMEM((tile, 2 * local_cols), jnp.bfloat16), pltpu.VMEM((tile, local_cols), jnp.bfloat16)],
        compiler_params=params,
        cost_estimate=pl.CostEstimate(
            flops=work * 400, bytes_accessed=work * 8, transcendentals=work * 6
        ),
        name="update",
    )(place, root_counts, features, root_sources, gain, matrix)
    return (factored, u_rows)


def solution(mesh):
    placed = (P(None, "row"), P(None, "col"), P("row", "col"), P("row"), P())
    return jax.shard_map(
        body,
        mesh=mesh,
        in_specs=placed,
        out_specs=(P("row", "col"), P(None, "col")),
        check_vma=False,
    )
```

```python
import functools
import math

import jax
import jax.numpy as jnp
from jax import lax
from jax.experimental import pallas as pl
from jax.experimental.pallas import tpu as pltpu
from jax.sharding import PartitionSpec as P

QUAD_MAX = 16
jump_factor = 4.0
disc_radius = 4.0

offset_x = [
    disc_radius * math.sqrt((q + 0.5) / QUAD_MAX) * math.cos(2.39996323 * q) for q in range(QUAD_MAX)
]
offset_y = [
    disc_radius * math.sqrt((q + 0.5) / QUAD_MAX) * math.sin(2.39996323 * q) for q in range(QUAD_MAX)
]


def summed(value, axis):
    count = lax.axis_size(axis)
    if count & (count - 1):
        return lax.psum(value, axis)
    distance = 1
    while distance < count:
        value = value + lax.ppermute(value, axis, [(i, i ^ distance) for i in range(count)])
        distance *= 2
    return value


def fill_tables(src_ref, table_x, table_y):
    size = src_ref[3:4, :]
    for q in range(QUAD_MAX):
        table_x[q : q + 1, :] = src_ref[0:1, :] + size * offset_x[q]
        table_y[q : q + 1, :] = src_ref[1:2, :] + size * offset_y[q]


def tile_sums(spread, rows, src_ref, table_x, table_y, count):
    point_x = spread[0, rows, :]
    point_y = spread[1, rows, :]
    delta_z = spread[2, rows, :] - src_ref[2:3, :]
    z_sq = delta_z * delta_z
    size = src_ref[3:4, :]
    base = z_sq + size * size
    shape = base.shape

    def add_point(q, sums):
        first, third = sums
        delta_x = point_x - table_x[pl.ds(q, 1), :]
        delta_y = point_y - table_y[pl.ds(q, 1), :]
        inverse = lax.rsqrt(delta_x * delta_x + delta_y * delta_y + base)
        return first + inverse, third + inverse * inverse * inverse

    def add_two(pair, sums):
        return add_point(2 * pair + 1, add_point(2 * pair, sums))

    zero = jnp.zeros(shape, jnp.float32)
    sums = add_two(0, (zero, zero))
    sums = lax.fori_loop(1, count // 2, add_two, sums)
    first, third = lax.fori_loop(count // 2 * 2, count, add_point, sums)
    weight = 1.0 / jnp.full((1, shape[1]), count, jnp.int32).astype(jnp.float32)
    return (2.0 * first + z_sq * third) * weight


def split_two(value):
    high = value.astype(jnp.bfloat16)
    low = (value - high.astype(jnp.float32)).astype(jnp.bfloat16)
    return high, low


def update_kernel(
    group, tile, jump, place_ref, own_counts_ref, root_counts_ref, feat_ref, own_ref, root_ref, gain_ref,
    out_ref, own_x, own_y, root_x, root_y, gain_wide, gain_high, spread, panel,
):
    step = pl.program_id(0)
    width = own_ref.shape[1]

    @pl.when(step == 0)
    def _():
        fill_tables(own_ref, own_x, own_y)
        fill_tables(root_ref, root_x, root_y)
        high, low = split_two(gain_ref[...])
        gain_wide[:, :width] = high
        gain_wide[:, width:] = low
        gain_high[...] = high

    for index in range(group):
        rows = pl.ds(index * tile, tile)
        columns = jnp.transpose(feat_ref[:, rows])
        for part in range(4):
            spread[part, rows, :] = jnp.broadcast_to(columns[:, part : part + 1], (tile, width))

    def one_tile(index, carry):
        rows = pl.ds(pl.multiple_of(index * tile, tile), tile)
        at = step * group + index
        out_ref[rows, :] = tile_sums(spread, rows, own_ref, own_x, own_y, own_counts_ref[at])
        panel[rows, :] = tile_sums(spread, rows, root_ref, root_x, root_y, root_counts_ref[at])
        return carry

    lax.fori_loop(0, group, one_tile, 0)

    keep = jnp.where(place_ref[0] == 0, 0.0, 1.0)
    lanes = lax.broadcasted_iota(jnp.int32, (1, width), 1)
    root_lanes = lanes.astype(jnp.float32)
    own_lanes = (lanes + place_ref[0]).astype(jnp.float32)
    for index in range(group):
        rows = pl.ds(index * tile, tile)
        element = spread[3, rows, :]
        high, low = split_two(panel[rows, :] + jnp.where(element == root_lanes, jump, 0.0))
        wide = jnp.dot(high, gain_wide[...], preferred_element_type=jnp.float32)
        small = jnp.dot(low, gain_high[...], preferred_element_type=jnp.float32)
        product = wide[:, :width] + (wide[:, width:] + small)
        own = out_ref[rows, :] + jnp.where(element == own_lanes, jump, 0.0)
        out_ref[rows, :] = keep * own + product


def pick_kernel(place_ref, pivots_ref, counts_ref, feat_ref, out_ref):
    side = out_ref.shape[1]
    local_rows = feat_ref.shape[1]
    lanes = lax.broadcasted_iota(jnp.int32, (8, side), 1)
    rows = lax.broadcasted_iota(jnp.int32, (8, 1), 0)

    def eight(turn, picked):
        for inner in range(8):
            number = turn * 8 + inner
            local = pivots_ref[number] - place_ref[1]
            present = jnp.where((local >= 0) & (local < local_rows), 1.0, 0.0)
            local = jnp.clip(local, 0, local_rows - 1)
            tile_id = local // side
            start = pl.multiple_of(tile_id * side, side)
            block = feat_ref[:, pl.ds(start, side)]
            value = jnp.sum(jnp.where(lanes == local - start, block, 0.0), axis=1, keepdims=True)
            value = jnp.where(rows == 4, counts_ref[tile_id].astype(jnp.float32), value)
            picked = jnp.where(lanes == number, value * present, picked)
        return picked

    out_ref[...] = lax.fori_loop(0, side // 8, eight, jnp.zeros((8, side), jnp.float32))


def pivot_matrix(columns, src_ref, counts):
    delta_x = columns[:, 0:1] - src_ref[0:1, :]
    delta_y = columns[:, 1:2] - src_ref[1:2, :]
    delta_z = columns[:, 2:3] - src_ref[2:3, :]
    size = src_ref[3:4, :]
    z_sq = delta_z * delta_z
    base = z_sq + size * size
    total = jnp.zeros_like(base)
    for q in range(QUAD_MAX):
        moved_x = delta_x - size * offset_x[q]
        moved_y = delta_y - size * offset_y[q]
        inverse = lax.rsqrt(moved_x * moved_x + moved_y * moved_y + base)
        weight = jnp.where(counts > q, 1.0 / counts, 0.0)
        total = total + weight * ((2.0 + z_sq * inverse * inverse) * inverse)
    return total


def eliminated(blocks, lanes, steps):
    rows = lax.broadcasted_iota(jnp.int32, (8, 1), 0)
    for column in steps:
        group, inner = divmod(column, 8)
        for blocks_of in blocks:
            pivot_row = blocks_of[group][inner : inner + 1, :]
            scale = 1.0 / pivot_row[:, column : column + 1]
            here = lanes == column
            right_row = jnp.where(here, 1.0, pivot_row)
            for index in range(group, len(blocks_of)):
                block = blocks_of[index]
                factor = block[:, column : column + 1] * scale
                if index == group:
                    under = rows > inner
                    factor = jnp.where(under, factor, 0.0)
                    cleared = jnp.where(here & under, 0.0, block)
                else:
                    cleared = jnp.where(here, 0.0, block)
                blocks_of[index] = cleared - factor * right_row
    return blocks


def panel_kernel(jump, place_ref, piv_ref, own_ref, root_ref, u_ref, gain_ref):
    side = piv_ref.shape[1]
    columns = jnp.transpose(piv_ref[...])
    rows = lax.broadcasted_iota(jnp.int32, (side, side), 0)
    cols = lax.broadcasted_iota(jnp.int32, (side, side), 1)
    diagonal = rows == cols
    is_root = place_ref[0] == 0
    identity = jnp.where(diagonal, 1.0, 0.0)
    square = pivot_matrix(columns, root_ref, columns[:, 4:5]) + jump * identity
    own = pivot_matrix(columns, own_ref, columns[:, 3:4]) + jnp.where(is_root, jump, 0.0) * identity
    lanes = lax.broadcasted_iota(jnp.int32, (1, side), 1)
    flipped = jnp.transpose(square)
    blocks = [
        [square[i : i + 8, :] for i in range(0, side, 8)],
        [flipped[i : i + 8, :] for i in range(0, side, 8)],
    ]
    blocks = eliminated(blocks, lanes, range(side))
    packed = jnp.concatenate(blocks[0], 0)
    packed_flipped = jnp.concatenate(blocks[1], 0)
    lower_inv = jnp.where(rows > cols, packed, identity)
    pivot_values = jnp.sum(jnp.where(diagonal, packed_flipped, 0.0), axis=1, keepdims=True)
    upper_inv = jnp.transpose(jnp.where(rows > cols, packed_flipped, identity) / pivot_values)
    u_rows = jnp.dot(
        lower_inv, own, precision=lax.Precision.HIGHEST, preferred_element_type=jnp.float32
    )
    u_ref[...] = u_rows
    gain = jnp.dot(
        upper_inv, u_rows, precision=lax.Precision.HIGHEST, preferred_element_type=jnp.float32
    )
    gain_ref[...] = jnp.where(is_root, upper_inv, -gain)


def body(colloc_points, sources, counts, row_element, pivots):
    tile = pivots.shape[0]
    local_rows = colloc_points.shape[1]
    local_cols = sources.shape[1]
    rows_tiles = local_rows // tile
    col_index = lax.axis_index("col")
    row_index = lax.axis_index("row")
    col_count = lax.axis_size("col")
    row_count = lax.axis_size("row")
    jump = jump_factor * tile
    own_counts = counts.reshape(-1)
    place = jnp.stack([col_index * local_cols, row_index * local_rows]).astype(jnp.int32)

    features = jnp.concatenate(
        [
            colloc_points,
            row_element.astype(jnp.float32)[None, :],
            jnp.zeros((4, local_rows), jnp.float32),
        ],
        0,
    )
    scalar = pl.BlockSpec(memory_space=pltpu.SMEM)
    whole = pl.BlockSpec(memory_space=pltpu.VMEM)
    params = pltpu.CompilerParams(vmem_limit_bytes=24 * 1024 * 1024)

    real_counts = own_counts.astype(jnp.float32)
    picked = pl.pallas_call(
        pick_kernel,
        out_shape=jax.ShapeDtypeStruct((8, tile), jnp.float32),
        in_specs=[scalar, scalar, scalar, whole],
        out_specs=whole,
        compiler_params=params,
        name="pick",
    )(place, pivots, own_counts, features)
    pivot_points = jnp.where(col_index == 0, picked[0:3], 0.0)
    pivot_counts = picked[4]
    root_sources = jnp.where((row_index == 0) & (col_index == 0), sources, 0.0)
    spread_counts = jnp.where(jnp.arange(col_count)[:, None] == col_index, pivot_counts[None, :], 0.0)
    padded = jnp.pad(real_counts, (0, -rows_tiles % tile))
    depth = padded.shape[0] // tile
    at_row = (jnp.arange(row_count)[:, None] == row_index) & (col_index == 0)
    root_counts = jnp.where(at_row, padded[None, :], 0.0).reshape(row_count * depth, tile)
    packed = jnp.concatenate([pivot_points, root_sources, spread_counts, root_counts], 0)
    known = summed(summed(packed, "col"), "row")
    pivot_points = known[0:3]
    root_sources = known[3:7]
    spread_counts = known[7 : 7 + col_count]
    own_pivot_counts = lax.dynamic_index_in_dim(spread_counts, col_index, 0)
    root_counts = known[7 + col_count :].reshape(row_count, depth * tile)
    root_counts = lax.dynamic_index_in_dim(root_counts, row_index, 0, keepdims=False)
    root_counts = jnp.round(root_counts[:rows_tiles]).astype(jnp.int32)
    pivot_info = jnp.concatenate(
        [pivot_points, own_pivot_counts, spread_counts[0:1], jnp.zeros((3, tile), jnp.float32)], 0
    )

    group = max(size for size in range(1, 9) if rows_tiles % size == 0)
    steps = rows_tiles // group
    feature_block = pl.BlockSpec((8, group * tile), lambda i: (0, i))
    matrix_block = pl.BlockSpec((group * tile, local_cols), lambda i: (i, 0))
    tables = [pltpu.VMEM((QUAD_MAX, local_cols), jnp.float32)] * 2
    block = jax.ShapeDtypeStruct((local_rows, local_cols), jnp.float32)
    work = local_rows * local_cols

    u_rows, gain = pl.pallas_call(
        functools.partial(panel_kernel, jump),
        out_shape=[jax.ShapeDtypeStruct((tile, local_cols), jnp.float32)] * 2,
        in_specs=[scalar, whole, whole, whole],
        out_specs=[whole, whole],
        compiler_params=params,
        name="panel",
    )(place, pivot_info, sources, root_sources)

    factored = pl.pallas_call(
        functools.partial(update_kernel, group, tile, jump),
        grid=(steps,),
        out_shape=block,
        in_specs=[scalar, scalar, scalar, feature_block, whole, whole, whole],
        out_specs=matrix_block,
        scratch_shapes=tables
        + tables
        + [
            pltpu.VMEM((tile, 2 * local_cols), jnp.bfloat16),
            pltpu.VMEM((tile, local_cols), jnp.bfloat16),
            pltpu.VMEM((4, group * tile, local_cols), jnp.float32),
            pltpu.VMEM((group * tile, local_cols), jnp.float32),
        ],
        compiler_params=params,
        cost_estimate=pl.CostEstimate(
            flops=work * 500, bytes_accessed=work * 4, transcendentals=work * 12
        ),
        name="update",
    )(place, own_counts, root_counts, features, sources, root_sources, gain)
    return (factored, u_rows)


def solution(mesh):
    placed = (P(None, "row"), P(None, "col"), P("row", "col"), P("row"), P())
    return jax.shard_map(
        body,
        mesh=mesh,
        in_specs=placed,
        out_specs=(P("row", "col"), P(None, "col")),
        check_vma=False,
    )
```
